32 devices in a mesh: groups: 2 (over y), rows: 4 (over z), sect: 4 (over x, core).
Axes of the slice: x: 2, y: 2, z: 4, core: 2. Of those that a mesh axis runs over, the one named last changes fastest.
Arguments:
- blocks: bfloat16 [128, 8, 256, 256], P(('rows', 'sect')), may hold values from -0.125 to 0.125
- col_index: int32 [128, 8], P(('rows', 'sect')), may hold values from 0 to 127, as said below
- counts: int32 [128], P(('rows', 'sect')), may hold values from 1 to 8, as said below
- shifts: float32 [4], P('groups'), parts along dimension 0, may hold values from 0.1 to 0.4
- vectors: float32 [64, 32768], P('groups', ('rows', 'sect')), parts along dimension 0, may hold values from -6 to 6
Outputs:
- krylov_block: float32 [64, 32768], P('groups', ('rows', 'sect')), parts along dimension 0
The draws below stay inside these ranges and needn't reach their ends.
There are 2 independent parts, one for each index of `groups`. The reference program is written for one: setup_inputs(seed, part) draws one part's arguments, and reference() takes and returns one part's arrays. A program takes and returns all parts, laid end to end along the dimension named above; an argument that names none is the same for every part. Nothing has to cross between parts.
Inputs may be any that keep to these rules, and one draw needn't show every extreme that they name: `col_index`: slot 0 of block row i names i itself. Every slot of block row (r, s, k) names a block row whose r differs from r by at most one; a thermal row names only thermal block rows. Duplicates may occur. `counts`: each aligned group of 16 block rows holds a row with all 8 slots live.
All inputs are finite; a program needn't handle non-finite values.
Results may differ from the reference program's by a relative error of at most 0.013.
Values may be sent and summed in bfloat16 or wider, within the bound.
A program may use at most 64 MiB of HBM per device.

```python
import jax
import jax.numpy as jnp
from jax import lax

BS = 256
COLS = 32
R_DEV = 8
NZ = 8
STEPS = 12
NB = 128
N_ROWS = 4
N_SECT = 4


def draw_col_index(key, part):
    key = jax.random.fold_in(key, 11)
    key_off, key_sect, key_loc = jax.random.split(key, 3)
    index_all = jnp.arange(NB, dtype=jnp.int32)[:, None]
    range_of = index_all // (N_SECT * R_DEV)
    sect_of = index_all // R_DEV % N_SECT
    offset = jax.random.randint(key_off, (NB, NZ), -1, 2, dtype=jnp.int32)
    target_range = jnp.clip(range_of + offset, 0, N_ROWS - 1)
    target_sect = jax.random.randint(key_sect, (NB, NZ), 0, N_SECT, dtype=jnp.int32)
    target_sect = jnp.where(sect_of == 0, 0, target_sect)
    target_loc = jax.random.randint(key_loc, (NB, NZ), 0, R_DEV, dtype=jnp.int32)
    target = (target_range * N_SECT + target_sect) * R_DEV + target_loc
    slot_ids = jnp.arange(NZ, dtype=jnp.int32)[None, :]
    return jnp.where(slot_ids == 0, index_all, target).astype(jnp.int32)


def draw_counts(key, part):
    key = jax.random.fold_in(key, 23)
    key_count, key_pick = jax.random.split(key)
    drawn = jax.random.randint(key_count, (NB,), 1, NZ + 1, dtype=jnp.int32)
    span = 2 * R_DEV
    number = NB // span
    picked = jax.random.randint(key_pick, (number,), 0, span, dtype=jnp.int32)
    index_all = jnp.arange(NB, dtype=jnp.int32)
    full_row = jnp.repeat(picked, span) == index_all % span
    return jnp.where(full_row, NZ, drawn).astype(jnp.int32)


def levels(own_key, extent, pieces, smallest, high):
    loudness, own = 1.0, jax.random.fold_in(own_key, 6)
    for position, blocks in pieces:
        heights = jnp.exp(jax.random.uniform(jax.random.fold_in(own, position), (blocks,), jnp.float32, smallest / len(pieces), high / len(pieces)))
        loudness = loudness * jnp.repeat(heights, extent[position] // blocks).reshape([-1 if axis == position else 1 for axis in range(len(extent))])
    return loudness


def normal_values(stream_key, extent, scale, bound, cuts=(), held_as=jnp.bfloat16):
    gain = levels(stream_key, extent, cuts, -0.22, 0.18) if cuts else 1.0
    result = jax.random.normal(stream_key, extent, jnp.float32) * scale * gain
    return jnp.minimum(jnp.maximum(result, -bound), bound).astype(held_as)


def setup_inputs(seed: int = 0, part: int = 0) -> dict:
    splits = jax.random.split(jax.random.key(seed), 6)
    part_splits = jax.random.split(jax.random.fold_in(splits[5], part), 6)
    return {
        "blocks": normal_values(splits[0], (NB, NZ, BS, BS), (NZ * BS) ** -0.5, 0.125, ((0, 16),)),
        "col_index": draw_col_index(jax.random.fold_in(splits[5], 71), part),
        "counts": draw_counts(jax.random.fold_in(splits[5], 71), part),
        "shifts": jnp.clip(jax.random.uniform(part_splits[3], (2,), jnp.float32, 0.1, 0.4), 0.1, 0.4),
        "vectors": normal_values(part_splits[4], (COLS, NB * BS), 1.0, 6.0, ((1, 16),), jnp.float32),
    }


def reference(blocks, col_index, counts, shifts, vectors):
    total = col_index.shape[0]
    stretch = R_DEV * N_SECT
    index_all = jnp.arange(total, dtype=jnp.int32)
    section = (index_all // R_DEV) % N_SECT
    shift_rows = jnp.where(section == 0, shifts[0], shifts[1])
    shift_dofs = jnp.repeat(shift_rows, BS)
    live = (jnp.arange(NZ, dtype=jnp.int32)[None, :] < counts[:, None]).astype(jnp.float32)

    def apply_once(current):
        narrow = current.astype(jnp.bfloat16)
        narrow = lax.optimization_barrier(narrow).astype(jnp.float32)
        blocked = narrow.reshape(COLS, total, BS)

        def one_group(group):
            picks = group * stretch + jnp.arange(stretch, dtype=jnp.int32)
            targets = jnp.take(col_index, picks, axis=0)
            chosen = jnp.take(blocked, targets.reshape(-1), axis=1).reshape(COLS, stretch, NZ, BS)
            chosen = chosen * jnp.take(live, picks, axis=0)[None, :, :, None]
            stored = jnp.take(blocks, picks, axis=0).astype(jnp.float32)
            return jnp.einsum("cqjb,qjab->qca", chosen, stored, precision=lax.Precision.HIGHEST)

        parts = lax.map(one_group, jnp.arange(total // stretch, dtype=jnp.int32))
        summed = jnp.transpose(parts.reshape(total, COLS, BS), (1, 0, 2)).reshape(COLS, total * BS)
        return summed + shift_dofs[None, :] * current

    current = vectors
    for applied in range(STEPS):
        current = apply_once(current)
    return current
```

```python
import functools

import jax
import jax.numpy as jnp
from jax import lax
from jax.experimental import pallas as pl
from jax.experimental.pallas import tpu as pltpu
from jax.sharding import PartitionSpec as P

STEPS = 12
CHUNKS = 2
VIA_ROWS = 5
KINDS = 15


def kernel(
    ranges,
    sections,
    slots,
    col_ref,
    counts_ref,
    shifts_ref,
    blocks_hbm,
    vec_ref,
    out_ref,
    blocks_ref,
    *scratch,
):
    windows = [scratch[2 * h : 2 * h + 2] for h in range(CHUNKS)]
    send_sem, recv_sem, load_sem = scratch[2 * CHUNKS :]
    rblk, _, width, _ = blocks_ref.shape
    ncols = vec_ref.shape[0]
    cols = ncols // CHUNKS
    z = lax.axis_index("rows")
    s = lax.axis_index("sect")
    partner = s + 1 - 2 * lax.rem(s, 2)
    across = lax.rem(s + 2, sections)
    has_below = z > 0
    has_above = z < ranges - 1
    stretch = sections * rblk
    zero_block = 3 * stretch
    base = (z - 1) * stretch
    via_rows = rblk * VIA_ROWS // 8

    loads = [
        pltpu.make_async_copy(blocks_hbm.at[k], blocks_ref.at[k], load_sem.at[k])
        for k in range(rblk)
    ]
    for load in loads:
        load.start()

    barrier = pltpu.get_barrier_semaphore()

    def greet(**device):
        pl.semaphore_signal(
            barrier, inc=1, device_id=device, device_id_type=pl.DeviceIdType.MESH
        )

    greet(sect=partner)
    greet(sect=across)
    pl.when(has_above)(lambda: greet(rows=z + 1))
    pl.when(has_below)(lambda: greet(rows=z - 1))

    shift = jnp.where(s == 0, shifts_ref[0], shifts_ref[1])

    whole = (0, rblk)
    upper = (0, via_rows)
    lower = (via_rows, rblk - via_rows)
    always = None
    to_partner = {"sect": partner}
    to_across = {"sect": across}
    to_above = {"rows": z + 1}
    to_below = {"rows": z - 1}
    table = {
        0: (always, always, to_partner, (1, s), whole, 1, (1, partner)),
        1: (always, always, to_across, (1, s), whole, 1, (1, across)),
        2: (has_above, has_below, to_above, (1, s), whole, 0, (0, s)),
        3: (has_below, has_above, to_below, (1, s), whole, 2, (2, s)),
        4: (always, always, to_partner, (1, across), whole, 1, (1, lax.rem(partner + 2, sections))),
        5: (has_above, has_below, to_above, (1, across), upper, 0, (0, across)),
        6: (has_below, has_above, to_below, (1, across), upper, 2, (2, across)),
        7: (has_below, has_below, to_partner, (0, s), whole, 0, (0, partner)),
        8: (has_above, has_above, to_partner, (2, s), whole, 2, (2, partner)),
        9: (has_below, has_below, to_across, (0, s), lower, 0, (0, across)),
        10: (has_above, has_above, to_across, (2, s), lower, 2, (2, across)),
        11: (has_below, has_below, to_partner, (0, across), upper, 0, (0, lax.rem(partner + 2, sections))),
        12: (has_above, has_above, to_partner, (2, across), upper, 2, (2, lax.rem(partner + 2, sections))),
        13: (has_below, has_below, to_partner, (0, across), lower, 0, (0, lax.rem(partner + 2, sections))),
        14: (has_above, has_above, to_partner, (2, across), lower, 2, (2, lax.rem(partner + 2, sections))),
    }

    def region(window, place, part):
        span, section = place
        first, count = part
        return window.at[pl.ds((span * sections + section) * rblk + first, count)]

    def guarded(condition, action):
        if condition is None:
            action()
        else:
            pl.when(condition)(action)

    def outgoing(h, par, kind):
        _, _, device, source, part, landing, _ = table[kind]
        window = windows[h][par]
        return pltpu.make_async_remote_copy(
            src_ref=region(window, source, part),
            dst_ref=region(window, (landing, source[1]), part),
            send_sem=send_sem.at[h, par, kind],
            recv_sem=recv_sem.at[h, par, kind],
            device_id=device,
            device_id_type=pl.DeviceIdType.MESH,
        )

    def send(h, par, *kinds):
        for kind in kinds:
            guarded(table[kind][0], lambda kind=kind: outgoing(h, par, kind).start())

    def sent(h, par):
        for kind in range(KINDS):
            guarded(table[kind][0], lambda kind=kind: outgoing(h, par, kind).wait_send())

    def received(h, par, *kinds):
        for kind in kinds:
            _, condition, device, _, part, _, place = table[kind]
            window = windows[h][par]

            def wait(kind=kind, place=place, part=part, device=device, window=window):
                pltpu.make_async_remote_copy(
                    src_ref=region(window, place, part),
                    dst_ref=region(window, place, part),
                    send_sem=send_sem.at[h, par, kind],
                    recv_sem=recv_sem.at[h, par, kind],
                    device_id=device,
                    device_id_type=pl.DeviceIdType.MESH,
                ).wait_recv()

            guarded(condition, wait)

    def relay_first(h, par):
        received(h, par, 1)
        send(h, par, 5, 6, 4)
        received(h, par, 2)
        send(h, par, 9, 7)
        received(h, par, 3)
        send(h, par, 10, 8)

    def relay_second(h, par):
        received(h, par, 5)
        send(h, par, 11)
        received(h, par, 6)
        send(h, par, 12)
        received(h, par, 9)
        send(h, par, 13)
        received(h, par, 10)
        send(h, par, 14)

    def gathered(h, par):
        received(h, par, 0, 4, 7, 8, 11, 12, 13, 14)

    def rows_of(h):
        return pl.ds(h * cols, cols)

    def apply_row(h, par, k):
        window = windows[h][par]
        here = pl.ds(pl.multiple_of(k * width, width), width)
        total = shift * out_ref[rows_of(h), here]
        for j in range(slots):
            position = jnp.where(j < counts_ref[k], col_ref[k, j] - base, zero_block)
            total += lax.dot_general(
                window[position],
                blocks_ref[k, j],
                (((1,), (1,)), ((), ())),
                preferred_element_type=jnp.float32,
            )
        out_ref[rows_of(h), here] = total
        windows[h][1 - par][stretch + s * rblk + k] = total.astype(jnp.bfloat16)

    def apply_rows(h, par, first, count):
        def body(k, carry):
            apply_row(h, par, k)
            return carry

        lax.fori_loop(first, first + count, body, 0, unroll=True)

    out_ref[...] = vec_ref[...]
    for h in range(CHUNKS):
        for par in range(2):
            windows[h][par][zero_block] = jnp.zeros((cols, width), jnp.bfloat16)
        for k in range(rblk):
            windows[h][0][stretch + s * rblk + k] = vec_ref[
                rows_of(h), pl.ds(k * width, width)
            ].astype(jnp.bfloat16)

    neighbours = 2 + has_below.astype(jnp.int32) + has_above.astype(jnp.int32)
    pl.semaphore_wait(barrier, neighbours)
    for h in range(CHUNKS):
        send(h, 0, 1, 2, 3, 0)
    for load in loads:
        load.wait()
    relay_first(0, 0)
    relay_second(0, 0)

    half = rblk // 2

    def two_steps(i, carry):
        for par in range(2):
            more = None if par == 0 else i < STEPS // 2 - 1
            for h in range(CHUNKS):
                last = h == CHUNKS - 1
                other, other_par = (0, 1 - par) if last else (h + 1, par)
                other_runs = more if last else None
                gathered(h, par)
                if CHUNKS > 1:
                    apply_rows(h, par, 0, half // 2)
                    guarded(other_runs, lambda: relay_first(other, other_par))
                    apply_rows(h, par, half // 2, rblk - half // 2 - half // 2)
                    guarded(other_runs, lambda: relay_second(other, other_par))
                    apply_rows(h, par, rblk - half // 2, half // 2)
                else:
                    apply_rows(h, par, 0, rblk)
                sent(h, par)
                guarded(more, lambda: send(h, 1 - par, 1, 2, 3, 0))
                if CHUNKS == 1:
                    guarded(more, lambda: relay_first(h, 1 - par))
                    guarded(more, lambda: relay_second(h, 1 - par))
        return carry

    lax.fori_loop(0, STEPS // 2, two_steps, 0)


def per_device(ranges, sections, blocks, col_index, counts, shifts, vectors):
    rblk, slots, width, _ = blocks.shape
    ncols = vectors.shape[0]
    window = pltpu.VMEM((3 * sections * rblk + 1, ncols // CHUNKS, width), jnp.bfloat16)
    smem = pl.BlockSpec(memory_space=pltpu.SMEM)
    vmem = pl.BlockSpec(memory_space=pltpu.VMEM)
    return pl.pallas_call(
        functools.partial(kernel, ranges, sections, slots),
        out_shape=jax.ShapeDtypeStruct(vectors.shape, jnp.float32),
        in_specs=[smem, smem, smem, pl.BlockSpec(memory_space=pl.ANY), vmem],
        out_specs=vmem,
        scratch_shapes=[
            pltpu.VMEM(blocks.shape, jnp.bfloat16),
            *[window] * (2 * CHUNKS),
            pltpu.SemaphoreType.DMA((CHUNKS, 2, KINDS)),
            pltpu.SemaphoreType.DMA((CHUNKS, 2, KINDS)),
            pltpu.SemaphoreType.DMA((rblk,)),
        ],
        compiler_params=pltpu.CompilerParams(
            collective_id=0, has_side_effects=True, vmem_limit_bytes=40 * 2**20
        ),
        cost_estimate=pl.CostEstimate(
            flops=2 * STEPS * ncols * blocks.size,
            bytes_accessed=2 * blocks.size + 8 * vectors.size,
            transcendentals=0,
        ),
    )(col_index, counts, shifts, blocks, vectors)


def solution(mesh):
    return jax.shard_map(
        functools.partial(per_device, mesh.shape["rows"], mesh.shape["sect"]),
        mesh=mesh,
        in_specs=(
            P(("rows", "sect"), None, None, None),
            P(("rows", "sect"), None),
            P(("rows", "sect")),
            P("groups"),
            P("groups", ("rows", "sect")),
        ),
        out_specs=P("groups", ("rows", "sect")),
        check_vma=False,
    )
```

```python
import functools

import jax
import jax.numpy as jnp
from jax import lax
from jax.experimental import pallas as pl
from jax.experimental.pallas import tpu as pltpu
from jax.sharding import PartitionSpec as P

STEPS = 12
KINDS = 13
GROUPS = 4
VIA_ROWS = (0, 2, 3)


def kernel(
    ranges,
    sections,
    slots,
    col_ref,
    counts_ref,
    shifts_ref,
    blocks_hbm,
    vec_ref,
    out_ref,
    blocks_ref,
    *scratch,
):
    windows = scratch[:2]
    send_sem, recv_sem, load_sem = scratch[2:]
    rblk, _, width, _ = blocks_ref.shape
    ncols = vec_ref.shape[0]
    count = rblk // GROUPS
    z = lax.axis_index("rows")
    s = lax.axis_index("sect")
    partner = s + 1 - 2 * lax.rem(s, 2)
    across = lax.rem(s + 2, sections)
    has_below = z > 0
    has_above = z < ranges - 1
    stretch = sections * rblk
    zero_block = 3 * stretch
    base = (z - 1) * stretch

    loads = [
        pltpu.make_async_copy(blocks_hbm.at[k], blocks_ref.at[k], load_sem.at[k])
        for k in range(rblk)
    ]
    for load in loads:
        load.start()

    barrier = pltpu.get_barrier_semaphore()

    def greet(**device):
        pl.semaphore_signal(
            barrier, inc=1, device_id=device, device_id_type=pl.DeviceIdType.MESH
        )

    greet(sect=partner)
    greet(sect=across)
    pl.when(has_above)(lambda: greet(rows=z + 1))
    pl.when(has_below)(lambda: greet(rows=z - 1))

    shift = jnp.where(s == 0, shifts_ref[0], shifts_ref[1])

    always = None
    diagonal = lax.rem(partner + 2, sections)
    to_partner = {"sect": partner}
    to_across = {"sect": across}
    to_above = {"rows": z + 1}
    to_below = {"rows": z - 1}
    table = (
        (always, always, to_partner, (1, s), 1, (1, partner)),
        (always, always, to_across, (1, s), 1, (1, across)),
        (has_above, has_below, to_above, (1, s), 0, (0, s)),
        (has_below, has_above, to_below, (1, s), 2, (2, s)),
        (always, always, to_partner, (1, across), 1, (1, diagonal)),
        (has_above, has_below, to_above, (1, across), 0, (0, across)),
        (has_below, has_above, to_below, (1, across), 2, (2, across)),
        (has_below, has_below, to_partner, (0, s), 0, (0, partner)),
        (has_above, has_above, to_partner, (2, s), 2, (2, partner)),
        (has_below, has_below, to_across, (0, s), 0, (0, across)),
        (has_above, has_above, to_across, (2, s), 2, (2, across)),
        (has_below, has_below, to_partner, (0, across), 0, (0, diagonal)),
        (has_above, has_above, to_partner, (2, across), 2, (2, diagonal)),
    )

    def region(par, span, section, g):
        return windows[par].at[pl.ds((span * sections + section) * rblk + g * count, count)]

    def guarded(condition, action):
        if condition is None:
            action()
        else:
            pl.when(condition)(action)

    def copy(par, kind, g, source, target):
        return pltpu.make_async_remote_copy(
            src_ref=source,
            dst_ref=target,
            send_sem=send_sem.at[par, kind, g],
            recv_sem=recv_sem.at[par, kind, g],
            device_id=table[kind][2],
            device_id_type=pl.DeviceIdType.MESH,
        )

    def outgoing(par, kind, g):
        _, _, _, (span, section), landing, _ = table[kind]
        return copy(par, kind, g, region(par, span, section, g), region(par, landing, section, g))

    def send(par, g, *kinds):
        for kind in kinds:
            guarded(table[kind][0], lambda kind=kind: outgoing(par, kind, g).start())

    def sent(par):
        for kind in range(KINDS):
            for g in range(GROUPS):
                if kind in (5, 6) and g not in VIA_ROWS or kind in (9, 10) and g in VIA_ROWS:
                    continue
                guarded(table[kind][0], lambda: outgoing(par, kind, g).wait_send())

    def received(par, g, *kinds):
        for kind in kinds:
            landed = region(par, *table[kind][5], g)
            guarded(
                table[kind][1], lambda: copy(par, kind, g, landed, landed).wait_recv()
            )

    def relay(par):
        for g in range(GROUPS):
            received(par, g, 1)
            if g in VIA_ROWS:
                send(par, g, 5, 6)
            send(par, g, 4)
            for kind, along, beside in ((2, 9, 7), (3, 10, 8)):
                received(par, g, kind)
                if g not in VIA_ROWS:
                    send(par, g, along)
                send(par, g, beside)
        for g in range(GROUPS):
            for kind, beside in zip((5, 6) if g in VIA_ROWS else (9, 10), (11, 12)):
                received(par, g, kind)
                send(par, g, beside)

    def gathered(par):
        for g in range(GROUPS):
            received(par, g, 0, 4, 7, 8, 11, 12)

    own = stretch + s * rblk

    def place(k):
        return pl.ds(k * width, width)

    def product(x, k, j):
        return lax.dot_general(
            x, blocks_ref[k, j], (((1,), (1,)), ((), ())), preferred_element_type=jnp.float32
        )

    def apply_self(par):
        for k in range(rblk):
            out_ref[:, place(k)] = shift * out_ref[:, place(k)] + product(
                windows[par][own + k], k, 0
            )

    def apply_others(par, k):
        total = out_ref[:, place(k)]
        for j in range(1, slots):
            position = jnp.where(j < counts_ref[k], col_ref[k, j] - base, zero_block)
            total += product(windows[par][position], k, j)
        out_ref[:, place(k)] = total
        windows[1 - par][own + k] = total.astype(jnp.bfloat16)

    out_ref[...] = vec_ref[...]
    for par in range(2):
        windows[par][zero_block] = jnp.zeros((ncols, width), jnp.bfloat16)
    for k in range(rblk):
        windows[0][own + k] = vec_ref[:, place(k)].astype(jnp.bfloat16)

    neighbours = 2 + has_below.astype(jnp.int32) + has_above.astype(jnp.int32)
    pl.semaphore_wait(barrier, neighbours)
    for g in range(GROUPS):
        send(0, g, 1, 2, 3, 0)
    relay(0)
    for load in loads:
        load.wait()
    apply_self(0)

    def two_steps(i, carry):
        for par in range(2):
            more = None if par == 0 else i < STEPS // 2 - 1
            gathered(par)
            for g in range(GROUPS):
                for k in range(g * count, (g + 1) * count):
                    apply_others(par, k)
                if g == GROUPS - 1:
                    sent(par)
                guarded(more, lambda: send(1 - par, g, 1, 2, 3, 0))
            guarded(more, lambda: apply_self(1 - par))
            guarded(more, lambda: relay(1 - par))
        return carry

    lax.fori_loop(0, STEPS // 2, two_steps, 0)


def per_device(ranges, sections, blocks, col_index, counts, shifts, vectors):
    rblk, slots, width, _ = blocks.shape
    ncols = vectors.shape[0]
    window = pltpu.VMEM((3 * sections * rblk + 1, ncols, width), jnp.bfloat16)
    smem = pl.BlockSpec(memory_space=pltpu.SMEM)
    vmem = pl.BlockSpec(memory_space=pltpu.VMEM)
    return pl.pallas_call(
        functools.partial(kernel, ranges, sections, slots),
        out_shape=jax.ShapeDtypeStruct(vectors.shape, jnp.float32),
        in_specs=[smem, smem, smem, pl.BlockSpec(memory_space=pl.ANY), vmem],
        out_specs=vmem,
        scratch_shapes=[
            pltpu.VMEM(blocks.shape, jnp.bfloat16),
            window,
            window,
            pltpu.SemaphoreType.DMA((2, KINDS, GROUPS)),
            pltpu.SemaphoreType.DMA((2, KINDS, GROUPS)),
            pltpu.SemaphoreType.DMA((rblk,)),
        ],
        compiler_params=pltpu.CompilerParams(
            collective_id=0, has_side_effects=True, vmem_limit_bytes=40 * 2**20
        ),
        cost_estimate=pl.CostEstimate(
            flops=2 * STEPS * ncols * blocks.size,
            bytes_accessed=2 * blocks.size + 8 * vectors.size,
            transcendentals=0,
        ),
    )(col_index, counts, shifts, blocks, vectors)


def solution(mesh):
    return jax.shard_map(
        functools.partial(per_device, mesh.shape["rows"], mesh.shape["sect"]),
        mesh=mesh,
        in_specs=(
            P(("rows", "sect"), None, None, None),
            P(("rows", "sect"), None),
            P(("rows", "sect")),
            P("groups"),
            P("groups", ("rows", "sect")),
        ),
        out_specs=P("groups", ("rows", "sect")),
        check_vma=False,
    )
```

```python
import functools

import jax
import jax.numpy as jnp
from jax import lax
from jax.experimental import pallas as pl
from jax.experimental.pallas import tpu as pltpu
from jax.sharding import PartitionSpec as P

STEPS = 12
KINDS = 15
ROUTES = "rrrr"
EIGHTHS = (2, 2, 2, 2)
GROUPS = len(ROUTES)
RELAYED = {"r": (5, 6), "s": (9, 10), "d": (13, 14)}


def kernel(
    ranges,
    sections,
    slots,
    col_ref,
    counts_ref,
    shifts_ref,
    blocks_hbm,
    vec_ref,
    out_ref,
    blocks_ref,
    *scratch,
):
    windows = scratch[:2]
    send_sem, recv_sem, partner_sem, load_sem = scratch[2:]
    rblk, _, width, _ = blocks_ref.shape
    ncols = vec_ref.shape[0]
    edges = [rblk * sum(EIGHTHS[:g]) // 8 for g in range(GROUPS + 1)]
    z = lax.axis_index("rows")
    s = lax.axis_index("sect")
    partner = s + 1 - 2 * lax.rem(s, 2)
    across = lax.rem(s + 2, sections)
    has_below = z > 0
    has_above = z < ranges - 1
    stretch = sections * rblk
    zero_block = 3 * stretch
    base = (z - 1) * stretch

    loads = [
        pltpu.make_async_copy(blocks_hbm.at[k], blocks_ref.at[k], load_sem.at[k])
        for k in range(rblk)
    ]
    for load in loads:
        load.start()

    barrier = pltpu.get_barrier_semaphore()

    def greet(**device):
        pl.semaphore_signal(
            barrier, inc=1, device_id=device, device_id_type=pl.DeviceIdType.MESH
        )

    greet(sect=partner)
    greet(sect=across)

    @pl.when(has_above)
    def _():
        greet(rows=z + 1)
        greet(rows=z + 1, sect=across)

    @pl.when(has_below)
    def _():
        greet(rows=z - 1)
        greet(rows=z - 1, sect=across)

    shift = jnp.where(s == 0, shifts_ref[0], shifts_ref[1])

    always = None
    diagonal = lax.rem(partner + 2, sections)
    to_partner = {"sect": partner}
    to_across = {"sect": across}
    to_above = {"rows": z + 1}
    to_below = {"rows": z - 1}
    table = (
        (always, always, to_partner, (1, s), 1, (1, partner)),
        (always, always, to_across, (1, s), 1, (1, across)),
        (has_above, has_below, to_above, (1, s), 0, (0, s)),
        (has_below, has_above, to_below, (1, s), 2, (2, s)),
        (always, always, to_partner, (1, across), 1, (1, diagonal)),
        (has_above, has_below, to_above, (1, across), 0, (0, across)),
        (has_below, has_above, to_below, (1, across), 2, (2, across)),
        (has_below, has_below, to_partner, (0, s), 0, (0, partner)),
        (has_above, has_above, to_partner, (2, s), 2, (2, partner)),
        (has_below, has_below, to_across, (0, s), 0, (0, across)),
        (has_above, has_above, to_across, (2, s), 2, (2, across)),
        (has_below, has_below, to_partner, (0, across), 0, (0, diagonal)),
        (has_above, has_above, to_partner, (2, across), 2, (2, diagonal)),
        (has_above, has_below, {"rows": z + 1, "sect": across}, (1, s), 0, (0, across)),
        (has_below, has_above, {"rows": z - 1, "sect": across}, (1, s), 2, (2, across)),
    )
    send_class = (0, 0, 1, 2, 0, 1, 2, 2, 1, 2, 1, 2, 1, 1, 2)
    partner_class = {0: 0, 4: 0, 7: 1, 11: 1, 8: 2, 12: 2}

    def region(par, span, section, g):
        return windows[par].at[pl.ds((span * sections + section) * rblk + edges[g], edges[g + 1] - edges[g])]

    def guarded(condition, action):
        if condition is None:
            action()
        else:
            pl.when(condition)(action)

    def copy(par, kind, g, source, target):
        return pltpu.make_async_remote_copy(
            src_ref=source,
            dst_ref=target,
            send_sem=send_sem.at[par, send_class[kind]],
            recv_sem=partner_sem.at[par, partner_class[kind]]
            if kind in partner_class
            else recv_sem.at[par, kind, g],
            device_id=table[kind][2],
            device_id_type=pl.DeviceIdType.MESH,
        )

    def outgoing(par, kind, g):
        _, _, _, (span, section), landing, _ = table[kind]
        return copy(par, kind, g, region(par, span, section, g), region(par, landing, section, g))

    def send(par, g, *kinds):
        for kind in kinds:
            guarded(table[kind][0], lambda kind=kind: outgoing(par, kind, g).start())

    def sent(par):
        for kind, pieces in ((0, 3), (2, 4), (3, 4)):
            everything = windows[par].at[pl.ds(0, pieces * rblk)]
            guarded(table[kind][0], lambda: copy(par, kind, 0, everything, everything).wait_send())

    def received(par, g, *kinds):
        for kind in kinds:
            landed = region(par, *table[kind][5], g)
            guarded(
                table[kind][1], lambda: copy(par, kind, g, landed, landed).wait_recv()
            )

    def start(par, g):
        send(par, g, 1, 2, 3, 0)
        if ROUTES[g] == "d":
            send(par, g, 13, 14)

    def relay(par):
        for g in range(GROUPS):
            received(par, g, 1)
            if ROUTES[g] == "r":
                send(par, g, 5, 6)
            if ROUTES[g] == "s":
                received(par, g, 2)
                send(par, g, 9)
                received(par, g, 3)
                send(par, g, 10)
        for g in range(GROUPS):
            send(par, g, 4)
            for kind, beside in ((2, 7), (3, 8)):
                if ROUTES[g] != "s":
                    received(par, g, kind)
                send(par, g, beside)
        for g in range(GROUPS):
            for kind, beside in zip(RELAYED[ROUTES[g]], (11, 12)):
                received(par, g, kind)
                send(par, g, beside)

    def gathered(par):
        for kind in (0, 7, 8):
            both = windows[par].at[pl.ds(0, 2 * rblk)]
            guarded(table[kind][1], lambda: copy(par, kind, 0, both, both).wait_recv())

    own = stretch + s * rblk

    def place(k):
        return pl.ds(k * width, width)

    def product(x, k, j):
        return lax.dot_general(
            x, blocks_ref[k, j], (((1,), (1,)), ((), ())), preferred_element_type=jnp.float32
        )

    def apply_self(par):
        for k in range(rblk):
            out_ref[:, place(k)] = shift * out_ref[:, place(k)] + product(
                windows[par][own + k], k, 0
            )

    def apply_others(par, k):
        total = out_ref[:, place(k)]
        for j in range(1, slots):
            position = jnp.where(j < counts_ref[k], col_ref[k, j] - base, zero_block)
            total += product(windows[par][position], k, j)
        out_ref[:, place(k)] = total
        windows[1 - par][own + k] = total.astype(jnp.bfloat16)

    out_ref[...] = vec_ref[...]
    for par in range(2):
        windows[par][zero_block] = jnp.zeros((ncols, width), jnp.bfloat16)
    for k in range(rblk):
        windows[0][own + k] = vec_ref[:, place(k)].astype(jnp.bfloat16)

    neighbours = 2 + 2 * (has_below.astype(jnp.int32) + has_above.astype(jnp.int32))
    pl.semaphore_wait(barrier, neighbours)
    for g in range(GROUPS):
        start(0, g)
    relay(0)
    for load in loads:
        load.wait()
    apply_self(0)

    def two_steps(i, carry):
        for par in range(2):
            more = None if par == 0 else i < STEPS // 2 - 1
            gathered(par)
            for g in range(GROUPS):
                for k in range(edges[g], edges[g + 1]):
                    apply_others(par, k)
                if g == GROUPS - 1:
                    sent(par)
                guarded(more, lambda: start(1 - par, g))
            guarded(more, lambda: apply_self(1 - par))
            guarded(more, lambda: relay(1 - par))
        return carry

    lax.fori_loop(0, STEPS // 2, two_steps, 0)


def per_device(ranges, sections, blocks, col_index, counts, shifts, vectors):
    rblk, slots, width, _ = blocks.shape
    ncols = vectors.shape[0]
    window = pltpu.VMEM((3 * sections * rblk + 1, ncols, width), jnp.bfloat16)
    smem = pl.BlockSpec(memory_space=pltpu.SMEM)
    vmem = pl.BlockSpec(memory_space=pltpu.VMEM)
    return pl.pallas_call(
        functools.partial(kernel, ranges, sections, slots),
        out_shape=jax.ShapeDtypeStruct(vectors.shape, jnp.float32),
        in_specs=[smem, smem, smem, pl.BlockSpec(memory_space=pl.ANY), vmem],
        out_specs=vmem,
        scratch_shapes=[
            pltpu.VMEM(blocks.shape, jnp.bfloat16),
            window,
            window,
            pltpu.SemaphoreType.DMA((2, 3)),
            pltpu.SemaphoreType.DMA((2, KINDS, GROUPS)),
            pltpu.SemaphoreType.DMA((2, 3)),
            pltpu.SemaphoreType.DMA((rblk,)),
        ],
        compiler_params=pltpu.CompilerParams(
            collective_id=0, has_side_effects=True, vmem_limit_bytes=40 * 2**20
        ),
        cost_estimate=pl.CostEstimate(
            flops=2 * STEPS * ncols * blocks.size,
            bytes_accessed=2 * blocks.size + 8 * vectors.size,
            transcendentals=0,
        ),
    )(col_index, counts, shifts, blocks, vectors)


def solution(mesh):
    return jax.shard_map(
        functools.partial(per_device, mesh.shape["rows"], mesh.shape["sect"]),
        mesh=mesh,
        in_specs=(
            P(("rows", "sect"), None, None, None),
            P(("rows", "sect"), None),
            P(("rows", "sect")),
            P("groups"),
            P("groups", ("rows", "sect")),
        ),
        out_specs=P("groups", ("rows", "sect")),
        check_vma=False,
    )
```
